32 devices in a mesh: vec: 4 (over x, core), dom: 8 (over z, y).
Axes of the slice: x: 2, y: 2, z: 4, core: 2. Of those that a mesh axis runs over, the one named last changes fastest.
Arguments:
- vectors: float32 [128, 64, 32, 128], P('vec', 'dom'), may hold values from -6 to 6
- coefficient: float32 [64, 32, 128], P('dom', 'vec'), may hold values from 0.25 to 2.5
- ritz: bfloat16 [64, 32, 128, 1024], P('dom', 'vec'), may hold values from -0.046875 to 0.046875
Outputs:
- residual: float32 [128, 64, 32, 128], P(None, 'dom', 'vec')
The draws below stay inside these ranges and needn't reach their ends.
All inputs are finite; a program needn't handle non-finite values.
Results may differ from the reference program's by a relative error of at most 0.003.
Values may be sent and summed in bfloat16 or wider, within the bound.
A program may use at most 128 MiB of HBM per device.

```python
import math
import jax
import jax.numpy as jnp
from jax import lax

VEC_DEV = 32
NY = 32
NX = 128
K = 1024
SWEEPS = 4
V = 128
NZ = 64


def level_of(rng, dims, split, least, high):
    def one(dim, blocks):
        steps = jax.random.uniform(jax.random.fold_in(jax.random.fold_in(rng, 6), dim), (blocks,), jnp.float32, least / len(split), high / len(split))
        return jnp.repeat(jnp.exp(steps), dims[dim] // blocks).reshape((-1,) + (1,) * (len(dims) - dim - 1))

    gain = one(*split[0])
    for cut in split[1:]:
        gain = gain * one(*cut)
    return gain


def bell_draw(own_key, shape, scale, limit, cuts=(), kind=jnp.bfloat16):
    result = scale * jax.random.normal(own_key, shape, jnp.float32)
    if cuts:
        result = result * level_of(own_key, shape, cuts, -0.22, 0.18)
    return jnp.clip(result, -limit, limit).astype(kind)


def setup_inputs(seed: int = 0) -> dict:
    seeds = jax.random.split(jax.random.key(seed), 4)
    return {
        "vectors": bell_draw(seeds[0], (V, NZ, NY, NX), 1.0, 6.0, ((0, 4), (1, 8)), jnp.float32),
        "coefficient": jnp.clip(jnp.exp(math.log(2.5) - 2.3025851 * jax.random.uniform(seeds[1], (NZ, NY, NX), jnp.float32) ** level_of(seeds[1], (NZ, NY, NX), ((0, 8), (1, 4)), -0.2, 0.2)), 0.25, 2.5),
        "ritz": bell_draw(seeds[2], (NZ, NY, NX, K), ((K * NX * NY * NZ) ** 0.5) ** -0.5, 0.046875, ((0, 8), (1, 4))),
    }


center_value = 7.125
half_range = 7.0


def scaled(field, coefficient):
    padded = jnp.pad(field, ((0, 0), (1, 1), (1, 1), (1, 1)))
    beside = padded[:, 2:, 1:-1, 1:-1] + padded[:, :-2, 1:-1, 1:-1]
    beside = beside + padded[:, 1:-1, 2:, 1:-1] + padded[:, 1:-1, :-2, 1:-1]
    beside = beside + padded[:, 1:-1, 1:-1, 2:] + padded[:, 1:-1, 1:-1, :-2]
    return ((6.0 + coefficient - center_value) * field - beside) / half_range


def filter_block(block, coefficient):
    previous = block
    current = scaled(block, coefficient)
    for sweep in range(SWEEPS - 1):
        previous, current = current, 2.0 * scaled(current, coefficient) - previous
    return current


def reference(vectors, coefficient, ritz):
    blocks = vectors.reshape(V // VEC_DEV, VEC_DEV, NZ, NY, NX)
    filtered = lax.map(lambda block: filter_block(block, coefficient), blocks).reshape(V, NZ * NY * NX)
    ritz_matrix = ritz.reshape(NZ * NY * NX, K)
    coeffs = jnp.dot(filtered.astype(jnp.bfloat16), ritz_matrix, preferred_element_type=jnp.float32)
    removed = lax.dot_general(coeffs.astype(jnp.bfloat16), ritz_matrix, (((1,), (1,)), ((), ())), preferred_element_type=jnp.float32)
    return (filtered - removed).reshape(V, NZ, NY, NX)
```

```python
import functools

import jax
import jax.numpy as jnp
from jax import lax
from jax.experimental import pallas as pl
from jax.experimental.pallas import tpu as pltpu
from jax.sharding import PartitionSpec as P

SWEEPS = 4
SUB = 8


center_value = 7.125
half_range = 7.0
MESH = pl.DeviceIdType.MESH


def padded_2(cells, sides, width):
    for axis, dim in sides:
        count = lax.axis_size(axis)
        ends = count - 1
        head = lax.slice_in_dim(cells, 0, width, axis=dim)
        tail = lax.slice_in_dim(cells, cells.shape[dim] - width, cells.shape[dim], axis=dim)
        cells = jnp.concatenate(
            [
                lax.ppermute(tail, axis, [(i, (i + 1) % count) for i in range(ends)]),
                cells,
                lax.ppermute(head, axis, [((i + 1) % count, i) for i in range(ends)]),
            ],
            axis=dim,
        )
    return cells


def side_sums(padded_z):
    inner = padded_z[:, 1:-1]
    beside = padded_z[:, 2:] + padded_z[:, :-2]
    padded = jnp.pad(inner, ((0, 0), (0, 0), (1, 1), (1, 1)))
    beside = beside + padded[:, :, 2:, 1:-1] + padded[:, :, :-2, 1:-1]
    beside = beside + padded[:, :, 1:-1, 2:] + padded[:, :, 1:-1, :-2]
    return (inner, beside)


def plain_body(vectors, coefficient, ritz):
    slab_coef = lax.all_gather(coefficient, "vec", axis=1, tiled=True)

    def scaled(field):
        padded_z = padded_2(field, (("dom", 1),), 1)
        inner, beside = side_sums(padded_z)
        return ((6.0 + slab_coef - center_value) * inner - beside) / half_range

    previous = vectors
    current = scaled(vectors)
    for sweep in range(SWEEPS - 1):
        previous, current = (current, 2.0 * scaled(current) - previous)
    cells = lax.all_to_all(current, "vec", split_axis=2, concat_axis=0, tiled=True)
    total_vectors = cells.shape[0]
    vec_matrix = cells.reshape(total_vectors, -1)
    ritz_matrix = ritz.reshape(vec_matrix.shape[1], ritz.shape[3])
    partial_value = jnp.dot(
        vec_matrix.astype(jnp.bfloat16), ritz_matrix, preferred_element_type=jnp.float32
    )
    coeffs = lax.psum(partial_value, ("vec", "dom"))
    removed = lax.dot_general(
        coeffs.astype(jnp.bfloat16),
        ritz_matrix,
        (((1,), (1,)), ((), ())),
        preferred_element_type=jnp.float32,
    )
    return (vec_matrix - removed).reshape(cells.shape)


def kernel(nv, nd, x_ref, coef_ref, ritz_ref, out_ref,
           low, halo, ext_a, ext_b, diag, coef_all, sendbuf, cells, lhs, ritz_v,
           acc, rs1, sum1, rs2, gathered, cmat,
           ritz_sem, coef_ss, coef_rs, halo_ss, halo_rs, a2a_ss, a2a_rs,
           r1_ss, r1_rs, r2_ss, r2_rs, g1_ss, g1_rs, g2_ss, g2_rs):
    H = SWEEPS
    chunks, slab, rows, nx = x_ref.shape
    ny = rows // SUB
    yb = ny // nv
    block = yb * SUB
    vb = acc.shape[1]
    total_rows = slab * yb
    iv = lax.axis_index("vec")
    idm = lax.axis_index("dom")
    at = lambda v, d: {"vec": v, "dom": d}

    def remote(src, dst, ss, rs, dev):
        return pltpu.make_async_remote_copy(src_ref=src, dst_ref=dst, send_sem=ss, recv_sem=rs, device_id=dev, device_id_type=MESH)

    ritz_copy = pltpu.make_async_copy(ritz_ref, ritz_v, ritz_sem)
    ritz_copy.start()

    barrier = pltpu.get_barrier_semaphore()
    me = iv * nd + idm
    for i in range(1, nv * nd):
        other = lax.rem(me + i, nv * nd)
        pl.semaphore_signal(barrier, inc=1, device_id=at(other // nd, lax.rem(other, nd)), device_id_type=MESH)
    pl.semaphore_wait(barrier, nv * nd - 1)

    has_lo = idm > 0
    has_hi = idm < nd - 1
    lo_dev = jnp.maximum(idm - 1, 0)
    hi_dev = jnp.minimum(idm + 1, nd - 1)

    peer = [lax.rem(iv + i, nv) for i in range(nv)]
    source = [lax.rem(iv + nv - i, nv) for i in range(nv)]

    def coef_copy(kind, i, who):
        if kind == 0:
            return remote(coef_ref, coef_all.at[who, pl.ds(H, slab)], coef_ss.at[0, i], coef_rs.at[0, i], at(peer[i], idm))
        if kind == 1:
            return remote(coef_ref.at[pl.ds(slab - H, H)], coef_all.at[who, pl.ds(0, H)], coef_ss.at[1, i], coef_rs.at[1, i], at(peer[i], hi_dev))
        return remote(coef_ref.at[pl.ds(0, H)], coef_all.at[who, pl.ds(H + slab, H)], coef_ss.at[2, i], coef_rs.at[2, i], at(peer[i], lo_dev))

    for i in range(1, nv):
        coef_copy(0, i, iv).start()

    @pl.when(has_hi)
    def _():
        for i in range(nv):
            coef_copy(1, i, iv).start()

    @pl.when(has_lo)
    def _():
        for i in range(nv):
            coef_copy(2, i, iv).start()

    def halo_copy(c, up):
        if up:
            return remote(low.at[c, pl.ds(slab - H, H)], halo.at[0, c], halo_ss.at[0, c], halo_rs.at[0, c], at(iv, hi_dev))
        return remote(low.at[c, pl.ds(0, H)], halo.at[1, c], halo_ss.at[1, c], halo_rs.at[1, c], at(iv, lo_dev))

    for c in range(chunks):
        @pl.loop(0, slab)
        def _(z):
            low[c, z] = x_ref[c, z].astype(jnp.bfloat16)

        @pl.when(has_hi)
        def _():
            halo_copy(c, True).start()

        @pl.when(has_lo)
        def _():
            halo_copy(c, False).start()

    coef_all[iv, pl.ds(H, slab)] = coef_ref[...]
    for i in range(1, nv):
        coef_copy(0, i, source[i]).wait_recv()

    @pl.when(has_lo)
    def _():
        for i in range(nv):
            coef_copy(1, i, source[i]).wait_recv()

    @pl.when(jnp.logical_not(has_lo))
    def _():
        for v in range(nv):
            coef_all[v, pl.ds(0, H)] = jnp.zeros((H, yb, nx), jnp.float32)

    @pl.when(has_hi)
    def _():
        for i in range(nv):
            coef_copy(2, i, source[i]).wait_recv()

    @pl.when(jnp.logical_not(has_hi))
    def _():
        for v in range(nv):
            coef_all[v, pl.ds(H + slab, H)] = jnp.zeros((H, yb, nx), jnp.float32)

    lo_on = has_lo.astype(jnp.float32)
    hi_on = has_hi.astype(jnp.float32)

    def valid(z):
        return jnp.where(z < H, lo_on, jnp.where(z >= H + slab, hi_on, 1.0))

    @pl.loop(0, slab + 2 * H)
    def _(z):
        on = valid(z) * (2.0 / half_range)
        for v in range(nv):
            term = (6.0 + coef_all[v, z] - center_value) * on
            for y in range(yb):
                diag[z, pl.ds((v * yb + y) * SUB, SUB), :] = jnp.broadcast_to(term[y:y + 1], (SUB, nx))

    lane = lax.broadcasted_iota(jnp.int32, (block, nx), 1)
    first = lane == 0
    last = lane == nx - 1

    def stencil(cur, z, b):
        on = valid(z) * (2.0 / half_range)
        r0 = b * block
        mid = cur[z, pl.ds(r0, block), :]
        zero = jnp.zeros((SUB, nx), jnp.float32)
        before = zero if b == 0 else cur[z, pl.ds(r0 - SUB, SUB), :]
        after = zero if b == nv - 1 else cur[z, pl.ds(r0 + block, SUB), :]
        beside = cur[z - 1, pl.ds(r0, block), :] + cur[z + 1, pl.ds(r0, block), :]
        beside += jnp.concatenate([before, mid[:-SUB]], axis=0) + jnp.concatenate([mid[SUB:], after], axis=0)
        beside += jnp.where(first, 0.0, pltpu.roll(mid, 1, 1)) + jnp.where(last, 0.0, pltpu.roll(mid, nx - 1, 1))
        return diag[z, pl.ds(r0, block), :] * mid - on * beside

    def a2a_copy(c, i, slot):
        return remote(sendbuf.at[c, peer[i]], cells.at[slot, c], a2a_ss.at[c, i], a2a_rs.at[c, i], at(peer[i], idm))

    for c in range(chunks):
        for side, there, base in ((0, has_lo, 0), (1, has_hi, H + slab)):
            @pl.when(there)
            def _():
                halo_copy(c, side == 0).wait_recv()
                for z in range(H):
                    ext_a[base + z] = halo[side, c, z].astype(jnp.float32)

            @pl.when(jnp.logical_not(there))
            def _():
                for z in range(H):
                    ext_a[base + z] = jnp.zeros((rows, nx), jnp.float32)

        @pl.loop(0, slab)
        def _(z):
            ext_a[H + z] = x_ref[c, z]

        for sweep in range(SWEEPS):
            cur, prev = (ext_a, ext_b) if sweep % 2 == 0 else (ext_b, ext_a)

            @pl.loop(sweep + 1, slab + 2 * H - 1 - sweep)
            def _(z):
                for b in range(nv):
                    value = stencil(cur, z, b)
                    r0 = b * block
                    if sweep == 0:
                        value = 0.5 * value
                    else:
                        value = value - prev[z, pl.ds(r0, block), :]
                    if sweep < SWEEPS - 1:
                        prev[z, pl.ds(r0, block), :] = value
                    else:
                        sendbuf[c, b, z - H] = value.astype(jnp.bfloat16)

        for i in range(1, nv):
            a2a_copy(c, i, iv).start()
        cells[iv, c] = sendbuf[c, iv]

    ritz_copy.wait()
    for c in range(chunks):
        for i in range(1, nv):
            a2a_copy(c, i, source[i]).wait_recv()

    @pl.loop(0, slab)
    def _(z):
        for y in range(0, yb, 2):
            parts = [
                cells[v, c, z, pl.ds(y * SUB, 2 * SUB), :].astype(jnp.float32)
                for v in range(nv) for c in range(chunks)
            ]
            for k in range(2):
                row = jnp.concatenate([p[k * SUB:(k + 1) * SUB] for p in parts], axis=0)
                place = pl.multiple_of((z * yb + y + k) * nx, nx)
                lhs[:, pl.ds(place, nx)] = row.astype(jnp.bfloat16)

    depth = yb * nx
    for v in range(nv):
        acc[v] = jnp.zeros(acc.shape[1:], jnp.float32)

    @pl.loop(0, slab)
    def _(z):
        place = pl.multiple_of(z * depth, depth)
        part = jnp.dot(lhs[:, pl.ds(place, depth)], ritz_v[pl.ds(place, depth), :], preferred_element_type=jnp.float32)
        for v in range(nv):
            acc[v] += part[v * vb:(v + 1) * vb]

    def r1_copy(i):
        return remote(acc.at[peer[i]], rs1.at[i - 1], r1_ss.at[i], r1_rs.at[i], at(peer[i], idm))

    for i in range(1, nv):
        r1_copy(i).start()
    for i in range(1, nv):
        r1_copy(i).wait_recv()
    total = acc[iv]
    for i in range(1, nv):
        total += rs1[i - 1]
    kb = sum1.shape[2]
    for d in range(nd):
        sum1[d] = total[:, d * kb:(d + 1) * kb]

    mate = [lax.rem(idm + i, nd) for i in range(nd)]
    origin = [lax.rem(idm + nd - i, nd) for i in range(nd)]

    def r2_copy(i):
        return remote(sum1.at[mate[i]], rs2.at[i - 1], r2_ss.at[i], r2_rs.at[i], at(iv, mate[i]))

    for i in range(1, nd):
        r2_copy(i).start()
    for i in range(1, nd):
        r2_copy(i).wait_recv()
    total = sum1[idm]
    for i in range(1, nd):
        total += rs2[i - 1]
    gathered[iv, idm] = total.astype(jnp.bfloat16)

    def g1_copy(i, d):
        return remote(gathered.at[iv, idm], gathered.at[iv, d], g1_ss.at[i], g1_rs.at[i], at(iv, mate[i]))

    for i in range(1, nd):
        g1_copy(i, idm).start()
    for i in range(1, nd):
        g1_copy(i, origin[i]).wait_recv()

    def g2_copy(i, v):
        return remote(gathered.at[iv], gathered.at[v], g2_ss.at[i], g2_rs.at[i], at(peer[i], idm))

    for i in range(1, nv):
        g2_copy(i, iv).start()
    for i in range(1, nv):
        g2_copy(i, source[i]).wait_recv()
    for v in range(nv):
        for d in range(nd):
            cmat[pl.ds(v * vb, vb), pl.ds(d * kb, kb)] = gathered[v, d]

    pair = 2 * nx

    @pl.loop(0, total_rows // 2)
    def _(r):
        place = pl.multiple_of(r * pair, pair)
        removed = lax.dot_general(
            cmat[...], ritz_v[pl.ds(place, pair), :], (((1,), (1,)), ((), ())), preferred_element_type=jnp.float32
        )
        out_ref[:, pl.ds(place, pair)] = lhs[:, pl.ds(place, pair)].astype(jnp.float32) - removed

    for i in range(1, nv):
        coef_copy(0, i, iv).wait_send()
        r1_copy(i).wait_send()
        g2_copy(i, iv).wait_send()
        for c in range(chunks):
            a2a_copy(c, i, iv).wait_send()
    for i in range(1, nd):
        r2_copy(i).wait_send()
        g1_copy(i, idm).wait_send()

    @pl.when(has_hi)
    def _():
        for i in range(nv):
            coef_copy(1, i, iv).wait_send()
        for c in range(chunks):
            halo_copy(c, True).wait_send()

    @pl.when(has_lo)
    def _():
        for i in range(nv):
            coef_copy(2, i, iv).wait_send()
        for c in range(chunks):
            halo_copy(c, False).wait_send()


def kernel_body(nv, nd, vectors, coefficient, ritz):
    vd, slab, ny, nx = vectors.shape
    kk = ritz.shape[3]
    yb = ny // nv
    chunks = vd // SUB
    rows = ny * SUB
    ext = slab + 2 * SWEEPS
    total = vd * nv
    cells = slab * yb * nx
    x = vectors.reshape(chunks, SUB, slab, ny, nx).transpose(0, 2, 3, 1, 4).reshape(chunks, slab, rows, nx)
    f32, b16 = jnp.float32, jnp.bfloat16
    dma = pltpu.SemaphoreType.DMA
    out = pl.pallas_call(
        functools.partial(kernel, nv, nd),
        out_shape=jax.ShapeDtypeStruct((total, cells), f32),
        in_specs=[
            pl.BlockSpec(memory_space=pltpu.VMEM),
            pl.BlockSpec(memory_space=pltpu.VMEM),
            pl.BlockSpec(memory_space=pl.ANY),
        ],
        out_specs=pl.BlockSpec(memory_space=pltpu.VMEM),
        scratch_shapes=[
            pltpu.VMEM((chunks, slab, rows, nx), b16),
            pltpu.VMEM((2, chunks, SWEEPS, rows, nx), b16),
            pltpu.VMEM((ext, rows, nx), f32),
            pltpu.VMEM((ext, rows, nx), f32),
            pltpu.VMEM((ext, rows, nx), f32),
            pltpu.VMEM((nv, ext, yb, nx), f32),
            pltpu.VMEM((chunks, nv, slab, yb * SUB, nx), b16),
            pltpu.VMEM((nv, chunks, slab, yb * SUB, nx), b16),
            pltpu.VMEM((total, cells), b16),
            pltpu.VMEM((cells, kk), b16),
            pltpu.VMEM((nv, vd, kk), f32),
            pltpu.VMEM((nv - 1, vd, kk), f32),
            pltpu.VMEM((nd, vd, kk // nd), f32),
            pltpu.VMEM((nd - 1, vd, kk // nd), f32),
            pltpu.VMEM((nv, nd, vd, kk // nd), b16),
            pltpu.VMEM((total, kk), b16),
            dma,
            dma((3, nv)), dma((3, nv)),
            dma((2, chunks)), dma((2, chunks)),
            dma((chunks, nv)), dma((chunks, nv)),
            dma((nv,)), dma((nv,)),
            dma((nd,)), dma((nd,)),
            dma((nd,)), dma((nd,)),
            dma((nv,)), dma((nv,)),
        ],
        compiler_params=pltpu.CompilerParams(
            collective_id=0, has_side_effects=True, vmem_limit_bytes=58 * 2**20
        ),
        cost_estimate=pl.CostEstimate(flops=4 * total * cells * kk, bytes_accessed=2 * cells * kk + 8 * total * cells, transcendentals=0),
    )(x, coefficient, ritz.reshape(cells, kk))
    return out.reshape(total, slab, yb, nx)


def body(nv, nd, vectors, coefficient, ritz):
    vd, slab, ny, nx = vectors.shape
    kk = ritz.shape[3]
    fits = (
        nv > 1 and nd > 1 and slab >= SWEEPS and vd % 16 == 0 and ny % (8 * nv) == 0
        and nx % 128 == 0 and kk % (128 * nd) == 0 and slab * (ny // nv) % 2 == 0
    )
    if fits:
        return kernel_body(nv, nd, vectors, coefficient, ritz)
    return plain_body(vectors, coefficient, ritz)


def solution(mesh):
    placed = (P("vec", "dom", None, None), P("dom", "vec", None), P("dom", "vec", None, None))
    return jax.shard_map(
        functools.partial(body, mesh.shape["vec"], mesh.shape["dom"]),
        mesh=mesh, in_specs=placed, out_specs=P(None, "dom", "vec", None), check_vma=False
    )
```

```python
import functools

import jax
import jax.numpy as jnp
from jax import lax
from jax.experimental import pallas as pl
from jax.experimental.pallas import tpu as pltpu
from jax.sharding import PartitionSpec as P

SWEEPS = 4
SUB = 8


center_value = 7.125
half_range = 7.0
MESH = pl.DeviceIdType.MESH


def padded_2(cells, sides, width):
    for axis, dim in sides:
        count = lax.axis_size(axis)
        ends = count - 1
        head = lax.slice_in_dim(cells, 0, width, axis=dim)
        tail = lax.slice_in_dim(cells, cells.shape[dim] - width, cells.shape[dim], axis=dim)
        cells = jnp.concatenate(
            [
                lax.ppermute(tail, axis, [(i, (i + 1) % count) for i in range(ends)]),
                cells,
                lax.ppermute(head, axis, [((i + 1) % count, i) for i in range(ends)]),
            ],
            axis=dim,
        )
    return cells


def side_sums(padded_z):
    inner = padded_z[:, 1:-1]
    beside = padded_z[:, 2:] + padded_z[:, :-2]
    padded = jnp.pad(inner, ((0, 0), (0, 0), (1, 1), (1, 1)))
    beside = beside + padded[:, :, 2:, 1:-1] + padded[:, :, :-2, 1:-1]
    beside = beside + padded[:, :, 1:-1, 2:] + padded[:, :, 1:-1, :-2]
    return (inner, beside)


def plain_body(vectors, coefficient, ritz):
    slab_coef = lax.all_gather(coefficient, "vec", axis=1, tiled=True)

    def scaled(field):
        padded_z = padded_2(field, (("dom", 1),), 1)
        inner, beside = side_sums(padded_z)
        return ((6.0 + slab_coef - center_value) * inner - beside) / half_range

    previous = vectors
    current = scaled(vectors)
    for sweep in range(SWEEPS - 1):
        previous, current = (current, 2.0 * scaled(current) - previous)
    cells = lax.all_to_all(current, "vec", split_axis=2, concat_axis=0, tiled=True)
    total_vectors = cells.shape[0]
    vec_matrix = cells.reshape(total_vectors, -1)
    ritz_matrix = ritz.reshape(vec_matrix.shape[1], ritz.shape[3])
    partial_value = jnp.dot(
        vec_matrix.astype(jnp.bfloat16), ritz_matrix, preferred_element_type=jnp.float32
    )
    coeffs = lax.psum(partial_value, ("vec", "dom"))
    removed = lax.dot_general(
        coeffs.astype(jnp.bfloat16),
        ritz_matrix,
        (((1,), (1,)), ((), ())),
        preferred_element_type=jnp.float32,
    )
    return (vec_matrix - removed).reshape(cells.shape)


def kernel(nv, nd, x_ref, coef_ref, ritz_ref, out_ref,
           x_in, xt, low, halo, ext_a, ext_b, diag, coef_all, sendbuf, cells, lhs, ritz_v,
           acc, rs1, sum1, rs2, gathered, cmat,
           x_sem, ritz_sem, coef_ss, coef_rs, halo_ss, halo_rs, a2a_ss, a2a_rs,
           r1_ss, r1_rs, r2_ss, r2_rs, g1_ss, g1_rs, g2_ss, g2_rs):
    H = SWEEPS
    vd, slab, ny, nx = x_ref.shape
    chunks, rows = vd // SUB, ny * SUB
    yb = ny // nv
    block = yb * SUB
    groups, vb = acc.shape[0], acc.shape[2]
    per = chunks // groups
    iv = lax.axis_index("vec")
    idm = lax.axis_index("dom")
    at = lambda v, d: {"vec": v, "dom": d}

    def remote(src, dst, ss, rs, dev):
        return pltpu.make_async_remote_copy(src_ref=src, dst_ref=dst, send_sem=ss, recv_sem=rs, device_id=dev, device_id_type=MESH)

    def x_copy(c):
        part = pl.ds(c * SUB, SUB)
        return pltpu.make_async_copy(x_ref.at[part], x_in.at[part], x_sem.at[c])

    for c in range(chunks):
        x_copy(c).start()
    ritz_copy = pltpu.make_async_copy(ritz_ref, ritz_v, ritz_sem)
    ritz_copy.start()

    barrier = pltpu.get_barrier_semaphore()
    me = iv * nd + idm
    for i in range(1, nv * nd):
        other = lax.rem(me + i, nv * nd)
        pl.semaphore_signal(barrier, inc=1, device_id=at(other // nd, lax.rem(other, nd)), device_id_type=MESH)
    pl.semaphore_wait(barrier, nv * nd - 1)

    has_lo = idm > 0
    has_hi = idm < nd - 1
    lo_dev = jnp.maximum(idm - 1, 0)
    hi_dev = jnp.minimum(idm + 1, nd - 1)

    peer = [lax.rem(iv + i, nv) for i in range(nv)]
    source = [lax.rem(iv + nv - i, nv) for i in range(nv)]

    def coef_copy(kind, i, who):
        if kind == 0:
            return remote(coef_ref, coef_all.at[who, pl.ds(H, slab)], coef_ss.at[0, i], coef_rs.at[0, i], at(peer[i], idm))
        if kind == 1:
            return remote(coef_ref.at[pl.ds(slab - H, H)], coef_all.at[who, pl.ds(0, H)], coef_ss.at[1, i], coef_rs.at[1, i], at(peer[i], hi_dev))
        return remote(coef_ref.at[pl.ds(0, H)], coef_all.at[who, pl.ds(H + slab, H)], coef_ss.at[2, i], coef_rs.at[2, i], at(peer[i], lo_dev))

    for i in range(1, nv):
        coef_copy(0, i, iv).start()

    @pl.when(has_hi)
    def _():
        for i in range(nv):
            coef_copy(1, i, iv).start()

    @pl.when(has_lo)
    def _():
        for i in range(nv):
            coef_copy(2, i, iv).start()

    def halo_copy(c, up):
        if up:
            return remote(low.at[c, pl.ds(slab - H, H)], halo.at[0, c], halo_ss.at[0, c], halo_rs.at[0, c], at(iv, hi_dev))
        return remote(low.at[c, pl.ds(0, H)], halo.at[1, c], halo_ss.at[1, c], halo_rs.at[1, c], at(iv, lo_dev))

    for c in range(chunks):
        x_copy(c).wait()

        @pl.loop(0, slab)
        def _(z):
            turned = jnp.transpose(x_in[pl.ds(c * SUB, SUB), z], (1, 0, 2)).reshape(rows, nx)
            xt[c, z] = turned
            low[c, z] = turned.astype(jnp.bfloat16)

        @pl.when(has_hi)
        def _():
            halo_copy(c, True).start()

        @pl.when(has_lo)
        def _():
            halo_copy(c, False).start()

    coef_all[iv, pl.ds(H, slab)] = coef_ref[...]
    for i in range(1, nv):
        coef_copy(0, i, source[i]).wait_recv()

    @pl.when(has_lo)
    def _():
        for i in range(nv):
            coef_copy(1, i, source[i]).wait_recv()

    @pl.when(jnp.logical_not(has_lo))
    def _():
        for v in range(nv):
            coef_all[v, pl.ds(0, H)] = jnp.zeros((H, yb, nx), jnp.float32)

    @pl.when(has_hi)
    def _():
        for i in range(nv):
            coef_copy(2, i, source[i]).wait_recv()

    @pl.when(jnp.logical_not(has_hi))
    def _():
        for v in range(nv):
            coef_all[v, pl.ds(H + slab, H)] = jnp.zeros((H, yb, nx), jnp.float32)

    lo_on = has_lo.astype(jnp.float32)
    hi_on = has_hi.astype(jnp.float32)

    def valid(z):
        return jnp.where(z < H, lo_on, jnp.where(z >= H + slab, hi_on, 1.0))

    @pl.loop(0, slab + 2 * H)
    def _(z):
        on = valid(z) * (2.0 / half_range)
        for v in range(nv):
            term = (6.0 + coef_all[v, z] - center_value) * on
            for y in range(yb):
                diag[z, pl.ds((v * yb + y) * SUB, SUB), :] = jnp.broadcast_to(term[y:y + 1], (SUB, nx))

    lane = lax.broadcasted_iota(jnp.int32, (block, nx), 1)
    first = lane == 0
    last = lane == nx - 1

    def stencil(cur, z, b):
        on = valid(z) * (2.0 / half_range)
        r0 = b * block
        mid = cur[z, pl.ds(r0, block), :]
        zero = jnp.zeros((SUB, nx), jnp.float32)
        before = zero if b == 0 else cur[z, pl.ds(r0 - SUB, SUB), :]
        after = zero if b == nv - 1 else cur[z, pl.ds(r0 + block, SUB), :]
        beside = cur[z - 1, pl.ds(r0, block), :] + cur[z + 1, pl.ds(r0, block), :]
        beside += jnp.concatenate([before, mid[:-SUB]], axis=0) + jnp.concatenate([mid[SUB:], after], axis=0)
        beside += jnp.where(first, 0.0, pltpu.roll(mid, 1, 1)) + jnp.where(last, 0.0, pltpu.roll(mid, nx - 1, 1))
        return diag[z, pl.ds(r0, block), :] * mid - on * beside

    def a2a_copy(c, i, slot):
        return remote(sendbuf.at[c, peer[i]], cells.at[slot, c], a2a_ss.at[c, i], a2a_rs.at[c, i], at(peer[i], idm))

    def filter_chunk(c):
        for side, there, base in ((0, has_lo, 0), (1, has_hi, H + slab)):
            @pl.when(there)
            def _():
                halo_copy(c, side == 0).wait_recv()
                for z in range(H):
                    ext_a[base + z] = halo[side, c, z].astype(jnp.float32)

            @pl.when(jnp.logical_not(there))
            def _():
                for z in range(H):
                    ext_a[base + z] = jnp.zeros((rows, nx), jnp.float32)

        @pl.loop(0, slab)
        def _(z):
            ext_a[H + z] = xt[c, z]

        for sweep in range(SWEEPS):
            cur, prev = (ext_a, ext_b) if sweep % 2 == 0 else (ext_b, ext_a)

            @pl.loop(sweep + 1, slab + 2 * H - 1 - sweep)
            def _(z):
                for b in range(nv):
                    value = stencil(cur, z, b)
                    r0 = b * block
                    if sweep == 0:
                        value = 0.5 * value
                    else:
                        value = value - prev[z, pl.ds(r0, block), :]
                    if sweep < SWEEPS - 1:
                        prev[z, pl.ds(r0, block), :] = value
                    else:
                        sendbuf[c, b, z - H] = value.astype(jnp.bfloat16)

        for i in range(1, nv):
            a2a_copy(c, i, iv).start()
        cells[iv, c] = sendbuf[c, iv]

    depth = yb * nx
    kb = sum1.shape[3]
    mate = [lax.rem(idm + i, nd) for i in range(nd)]
    origin = [lax.rem(idm + nd - i, nd) for i in range(nd)]

    def first_product(g):
        for c in range(g * per, (g + 1) * per):
            for i in range(1, nv):
                a2a_copy(c, i, source[i]).wait_recv()

        @pl.loop(0, slab)
        def _(z):
            for y in range(0, yb, 2):
                parts = [
                    cells[v, c, z, pl.ds(y * SUB, 2 * SUB), :].astype(jnp.float32)
                    for v in range(nv) for c in range(g * per, (g + 1) * per)
                ]
                for k in range(2):
                    row = jnp.concatenate([p[k * SUB:(k + 1) * SUB] for p in parts], axis=0)
                    place = pl.multiple_of((z * yb + y + k) * nx, nx)
                    lhs[g, :, pl.ds(place, nx)] = row.astype(jnp.bfloat16)

        for v in range(nv):
            acc[g, v] = jnp.zeros(acc.shape[2:], jnp.float32)

        @pl.loop(0, slab)
        def _(z):
            place = pl.multiple_of(z * depth, depth)
            part = jnp.dot(lhs[g, :, pl.ds(place, depth)], ritz_v[pl.ds(place, depth), :], preferred_element_type=jnp.float32)
            for v in range(nv):
                acc[g, v] += part[v * vb:(v + 1) * vb]

        for i in range(1, nv):
            r1_copy(g, i).start()

    def r1_copy(g, i):
        return remote(acc.at[g, peer[i]], rs1.at[g, i - 1], r1_ss.at[g, i], r1_rs.at[g, i], at(peer[i], idm))

    def r2_copy(g, i):
        return remote(sum1.at[g, mate[i]], rs2.at[g, i - 1], r2_ss.at[g, i], r2_rs.at[g, i], at(iv, mate[i]))

    def g1_copy(g, i, d):
        return remote(gathered.at[g, iv, idm], gathered.at[g, iv, d], g1_ss.at[g, i], g1_rs.at[g, i], at(iv, mate[i]))

    def g2_copy(g, i, v):
        return remote(gathered.at[g, iv], gathered.at[g, v], g2_ss.at[g, i], g2_rs.at[g, i], at(peer[i], idm))

    def sum_vec(g):
        for i in range(1, nv):
            r1_copy(g, i).wait_recv()
        total = acc[g, iv]
        for i in range(1, nv):
            total += rs1[g, i - 1]
        for d in range(nd):
            sum1[g, d] = total[:, d * kb:(d + 1) * kb]
        for i in range(1, nd):
            r2_copy(g, i).start()

    def sum_dom(g):
        for i in range(1, nd):
            r2_copy(g, i).wait_recv()
        total = sum1[g, idm]
        for i in range(1, nd):
            total += rs2[g, i - 1]
        gathered[g, iv, idm] = total.astype(jnp.bfloat16)
        for i in range(1, nd):
            g1_copy(g, i, idm).start()

    def gather_dom(g):
        for i in range(1, nd):
            g1_copy(g, i, origin[i]).wait_recv()
        for i in range(1, nv):
            g2_copy(g, i, iv).start()

    def second_product():
        for g in range(groups):
            for i in range(1, nv):
                g2_copy(g, i, source[i]).wait_recv()
            for v in range(nv):
                for d in range(nd):
                    cmat[pl.ds(g * nv * vb + v * vb, vb), pl.ds(d * kb, kb)] = gathered[g, v, d]

        @pl.loop(0, slab)
        def _(r):
            place = pl.multiple_of(r * depth, depth)
            removed = lax.dot_general(
                cmat[...], ritz_v[pl.ds(place, depth), :], (((1,), (1,)), ((), ())), preferred_element_type=jnp.float32
            )
            for g in range(groups):
                kept = lhs[g, :, pl.ds(place, depth)].astype(jnp.float32) - removed[g * nv * vb:(g + 1) * nv * vb]
                for v in range(nv):
                    out_ref[pl.ds(v * vd + g * vb, vb), pl.ds(place, depth)] = kept[v * vb:(v + 1) * vb]

    for c in range(chunks - 1):
        filter_chunk(c)
    ritz_copy.wait()
    filter_chunk(chunks - 1)
    first_product(0)
    first_product(1)
    sum_vec(0)
    sum_dom(0)
    sum_vec(1)
    gather_dom(0)
    sum_dom(1)
    gather_dom(1)
    second_product()

    for i in range(1, nv):
        coef_copy(0, i, iv).wait_send()
        for g in range(groups):
            r1_copy(g, i).wait_send()
            g2_copy(g, i, iv).wait_send()
        for c in range(chunks):
            a2a_copy(c, i, iv).wait_send()
    for i in range(1, nd):
        for g in range(groups):
            r2_copy(g, i).wait_send()
            g1_copy(g, i, idm).wait_send()

    @pl.when(has_hi)
    def _():
        for i in range(nv):
            coef_copy(1, i, iv).wait_send()
        for c in range(chunks):
            halo_copy(c, True).wait_send()

    @pl.when(has_lo)
    def _():
        for i in range(nv):
            coef_copy(2, i, iv).wait_send()
        for c in range(chunks):
            halo_copy(c, False).wait_send()


def kernel_body(nv, nd, vectors, coefficient, ritz):
    vd, slab, ny, nx = vectors.shape
    kk = ritz.shape[3]
    yb = ny // nv
    chunks = vd // SUB
    rows = ny * SUB
    ext = slab + 2 * SWEEPS
    total = vd * nv
    cells = slab * yb * nx
    groups = 2
    vb = vd // groups
    f32, b16 = jnp.float32, jnp.bfloat16
    dma = pltpu.SemaphoreType.DMA
    out = pl.pallas_call(
        functools.partial(kernel, nv, nd),
        out_shape=jax.ShapeDtypeStruct((total, cells), f32),
        in_specs=[
            pl.BlockSpec(memory_space=pl.ANY),
            pl.BlockSpec(memory_space=pltpu.VMEM),
            pl.BlockSpec(memory_space=pl.ANY),
        ],
        out_specs=pl.BlockSpec(memory_space=pltpu.VMEM),
        scratch_shapes=[
            pltpu.VMEM(vectors.shape, f32),
            pltpu.VMEM((chunks, slab, rows, nx), f32),
            pltpu.VMEM((chunks, slab, rows, nx), b16),
            pltpu.VMEM((2, chunks, SWEEPS, rows, nx), b16),
            pltpu.VMEM((ext, rows, nx), f32),
            pltpu.VMEM((ext, rows, nx), f32),
            pltpu.VMEM((ext, rows, nx), f32),
            pltpu.VMEM((nv, ext, yb, nx), f32),
            pltpu.VMEM((chunks, nv, slab, yb * SUB, nx), b16),
            pltpu.VMEM((nv, chunks, slab, yb * SUB, nx), b16),
            pltpu.VMEM((groups, total // groups, cells), b16),
            pltpu.VMEM((cells, kk), b16),
            pltpu.VMEM((groups, nv, vb, kk), f32),
            pltpu.VMEM((groups, nv - 1, vb, kk), f32),
            pltpu.VMEM((groups, nd, vb, kk // nd), f32),
            pltpu.VMEM((groups, nd - 1, vb, kk // nd), f32),
            pltpu.VMEM((groups, nv, nd, vb, kk // nd), b16),
            pltpu.VMEM((total, kk), b16),
            dma((chunks,)), dma,
            dma((3, nv)), dma((3, nv)),
            dma((2, chunks)), dma((2, chunks)),
            dma((chunks, nv)), dma((chunks, nv)),
            dma((groups, nv)), dma((groups, nv)),
            dma((groups, nd)), dma((groups, nd)),
            dma((groups, nd)), dma((groups, nd)),
            dma((groups, nv)), dma((groups, nv)),
        ],
        compiler_params=pltpu.CompilerParams(
            collective_id=0, has_side_effects=True, vmem_limit_bytes=58 * 2**20
        ),
        cost_estimate=pl.CostEstimate(flops=4 * total * cells * kk, bytes_accessed=2 * cells * kk + 8 * total * cells, transcendentals=0),
    )(vectors, coefficient, ritz.reshape(cells, kk))
    return out.reshape(total, slab, yb, nx)


def body(nv, nd, vectors, coefficient, ritz):
    vd, slab, ny, nx = vectors.shape
    kk = ritz.shape[3]
    fits = (
        nv > 1 and nd > 1 and slab >= SWEEPS and vd % 32 == 0 and ny % (8 * nv) == 0
        and nx % 128 == 0 and kk % (128 * nd) == 0 and slab * (ny // nv) % 2 == 0
    )
    if fits:
        return kernel_body(nv, nd, vectors, coefficient, ritz)
    return plain_body(vectors, coefficient, ritz)


def solution(mesh):
    placed = (P("vec", "dom", None, None), P("dom", "vec", None), P("dom", "vec", None, None))
    return jax.shard_map(
        functools.partial(body, mesh.shape["vec"], mesh.shape["dom"]),
        mesh=mesh, in_specs=placed, out_specs=P(None, "dom", "vec", None), check_vma=False
    )
```
